512 devices in a mesh: dp: 32 (over z, core), mp: 16 (over x, y).
Axes of the slice: x: 4, y: 4, z: 16, core: 2. Of those that a mesh axis runs over, the one named last changes fastest.
Arguments:
- tokens: bfloat16 [4096, 4096], P('dp', 'mp'), may hold values from -55 to 55
- encodings: bfloat16 [16384, 896], P('dp'), may hold values from -6 to 6
- shard_place: int32 [32, 512], P('dp'), may hold values from 0 to 511, each once within a row
- owner_map: int32 [32, 512], P('dp'), may hold values from 0 to 511, each once within a row
- query_weight: bfloat16 [4096, 2048], P('dp', 'mp'), may hold values from -0.09375 to 0.09375
- key_weight: bfloat16 [896, 2048], P('dp', 'mp'), may hold values from -0.1875 to 0.1875
- value_weight: bfloat16 [896, 2048], P('dp', 'mp'), may hold values from -0.1875 to 0.1875
- out_weight: bfloat16 [2048, 4096], P('mp', 'dp'), may hold values from -0.125 to 0.125
- grad_out: bfloat16 [4096, 4096], P('dp', 'mp'), may hold values from -6 to 6
Outputs:
- layer_out: bfloat16 [4096, 4096], P('dp')
- input_grad: bfloat16 [4096, 4096], P('dp', 'mp')
- query_grad: bfloat16 [4096, 2048], P('dp', 'mp')
- key_grad: bfloat16 [896, 2048], P('dp', 'mp')
- value_grad: bfloat16 [896, 2048], P('dp', 'mp')
- out_grad: bfloat16 [2048, 4096], P('mp', 'dp')
- encoding_grad: bfloat16 [16384, 896], P('dp')
The draws below stay inside these ranges and needn't reach their ends.
Inputs may be any that keep to these rules, and one draw needn't show every extreme that they name: `shard_place`: each row is an ordering of 0 to 511. `owner_map`: each row is an ordering of 0 to 511.
All inputs are finite; a program needn't handle non-finite values.
Results may differ from the reference program's by a relative error of at most 0.034.
Values may be sent and summed in bfloat16 or wider, within the bound.
A program may use at most 64 MiB of HBM per device.

```python
import jax
import jax.numpy as jnp
from jax import lax

D = 4096
HEADS = 16
HDIM = 128
ENC = 896
STRETCH = 64
NEIGH = 2
NLEN = 128
ROWS_DEV = 512
TOKENS = 4096
NROWS = 16384
INNER = 2048
SHARDS = 32
PEER = 16
SEQ_LEN = 2048
N_MP = 16


def draw_tokens(key, part):
    key = jax.random.fold_in(key, 11)
    base_key = jax.random.fold_in(key, 0)
    values = jnp.clip(jax.random.normal(base_key, (TOKENS, D), jnp.float32), -6.0, 6.0)
    return values.astype(jnp.bfloat16)


def steps_of(rng, shape, pieces, least, top_value):
    def one(axis_at, parts):
        steps = jax.random.uniform(jax.random.fold_in(jax.random.fold_in(rng, 6), axis_at), (parts,), jnp.float32, least / len(pieces), top_value / len(pieces))
        return jnp.repeat(jnp.exp(steps), shape[axis_at] // parts).reshape((-1,) + (1,) * (len(shape) - axis_at - 1))

    loudness = one(*pieces[0])
    for cut in pieces[1:]:
        loudness = loudness * one(*cut)
    return loudness


def centred(key, shape, scale, limit, cuts=(), kind=jnp.bfloat16):
    values = jax.random.normal(key, shape, jnp.float32) * scale
    if len(cuts) > 0:
        values = steps_of(key, shape, cuts, -0.22, 0.18) * values
    return jnp.clip(values, min=-limit, max=limit).astype(kind)


def setup_inputs(seed: int = 0) -> dict:
    seeds = jax.random.split(jax.random.key(seed), 10)
    tokens = draw_tokens(jax.random.fold_in(seeds[9], 71), 0)
    encodings = centred(seeds[1], (NROWS, ENC), 1.0, 6.0, ((0, 32),))
    shard_place = jax.vmap(lambda own: jax.random.permutation(own, ROWS_DEV))(jax.random.split(seeds[2], SHARDS)).reshape((SHARDS, ROWS_DEV)).astype(jnp.int32)
    owner_map = jax.vmap(lambda own: jax.random.permutation(own, ROWS_DEV))(jax.random.split(seeds[3], SHARDS)).reshape((SHARDS, ROWS_DEV)).astype(jnp.int32)
    query_weight = centred(seeds[4], (D, INNER), D ** -0.5, 0.09375, ((0, 32), (1, 16)))
    key_weight = centred(seeds[5], (ENC, INNER), ENC ** -0.5, 0.1875, ((0, 32), (1, 16)))
    value_weight = centred(seeds[6], (ENC, INNER), ENC ** -0.5, 0.1875, ((0, 32), (1, 16)))
    out_weight = centred(seeds[7], (INNER, D), INNER ** -0.5, 0.125, ((0, 16), (1, 32)))
    grad_out = centred(seeds[8], (TOKENS, D), 1.0, 6.0, ((0, 32), (1, 16)))
    return {"tokens": tokens, "encodings": encodings, "shard_place": shard_place, "owner_map": owner_map, "query_weight": query_weight, "key_weight": key_weight, "value_weight": value_weight, "out_weight": out_weight, "grad_out": grad_out}


def relay_rows(encodings, shard_place, owner_map):
    source = owner_map // PEER
    slot_pos = owner_map % PEER
    target = jnp.arange(SHARDS, dtype=jnp.int32)[:, None]
    local_rows = shard_place[source, target * PEER + slot_pos]
    source_rows = (source * ROWS_DEV + local_rows).reshape(-1).astype(jnp.int32)
    return encodings[source_rows], source_rows


def stretch_mask(stretch_count):
    stretch_start = jnp.arange(stretch_count, dtype=jnp.int32)[:, None] * STRETCH
    token_pos = stretch_start + STRETCH - 1 + jnp.arange(STRETCH, dtype=jnp.int32)[None, :]
    inside = (token_pos < TOKENS) & (token_pos // SEQ_LEN == stretch_start // SEQ_LEN)
    return inside.astype(jnp.float32)


def to_stretches(token_rows, stretch_count):
    padding = jnp.zeros((STRETCH - 1, INNER), token_rows.dtype)
    moved = jnp.concatenate([token_rows[STRETCH - 1:], padding], 0)
    return moved.reshape(stretch_count, STRETCH, HEADS, HDIM).astype(jnp.float32)


def from_stretches(block_rows):
    flat_rows = block_rows.reshape(TOKENS, INNER)
    padding = jnp.zeros((STRETCH - 1, INNER), flat_rows.dtype)
    return jnp.concatenate([padding, flat_rows[:TOKENS - STRETCH + 1]], 0)


def group_sum(factor_pairs, part_count):
    group_cols = factor_pairs[0][0].shape[1] // part_count
    out_shape = (factor_pairs[0][0].shape[0], factor_pairs[0][1].shape[1])

    def add_group(running, group):
        partial_value = jnp.zeros(out_shape, jnp.float32)
        for left_rows, right_rows in factor_pairs:
            left_part = lax.dynamic_slice_in_dim(left_rows, group * group_cols, group_cols, 1)
            right_part = lax.dynamic_slice_in_dim(right_rows, group * group_cols, group_cols, 0)
            partial_value = partial_value + jnp.dot(left_part, right_part, preferred_element_type=jnp.float32)
        rounded = lax.optimization_barrier(partial_value.astype(jnp.bfloat16))
        return running + rounded.astype(jnp.float32), None

    running, _ = lax.scan(add_group, jnp.zeros(out_shape, jnp.float32), jnp.arange(part_count, dtype=jnp.int32))
    return running


def block_sum(left_rows, right_rows, part_count):
    block_rows = left_rows.shape[0] // part_count
    out_shape = (left_rows.shape[1], right_rows.shape[1])

    def add_block(running, block):
        left_part = lax.dynamic_slice_in_dim(left_rows, block * block_rows, block_rows, 0)
        right_part = lax.dynamic_slice_in_dim(right_rows, block * block_rows, block_rows, 0)
        partial_value = jnp.dot(left_part.T, right_part, preferred_element_type=jnp.float32)
        rounded = lax.optimization_barrier(partial_value.astype(jnp.bfloat16))
        return running + rounded.astype(jnp.float32), None

    running, _ = lax.scan(add_block, jnp.zeros(out_shape, jnp.float32), jnp.arange(part_count, dtype=jnp.int32))
    return running


def reference(tokens, encodings, shard_place, owner_map, query_weight, key_weight, value_weight, out_weight, grad_out):
    score_scale = HDIM ** -0.5
    stretch_count = TOKENS // STRETCH
    stretch_keys = NEIGH * NLEN
    neighbours, source_rows = relay_rows(encodings, shard_place, owner_map)
    queries = jnp.dot(tokens, query_weight, preferred_element_type=jnp.float32).astype(jnp.bfloat16)
    keys_all = jnp.dot(neighbours, key_weight, preferred_element_type=jnp.float32).astype(jnp.bfloat16)
    values_all = jnp.dot(neighbours, value_weight, preferred_element_type=jnp.float32).astype(jnp.bfloat16)
    inside = stretch_mask(stretch_count)[:, :, None, None]
    query_blocks = to_stretches(queries, stretch_count)
    key_blocks = keys_all.reshape(stretch_count, stretch_keys, HEADS, HDIM).astype(jnp.float32)
    value_blocks = values_all.reshape(stretch_count, stretch_keys, HEADS, HDIM).astype(jnp.float32)
    scores = jnp.einsum("gqhd,gkhd->ghqk", query_blocks, key_blocks) * score_scale
    row_top = jnp.max(scores, -1, keepdims=True)
    expo_terms = jnp.exp(scores - row_top)
    soft_probs = expo_terms / jnp.sum(expo_terms, -1, keepdims=True)
    probs_half = lax.optimization_barrier(soft_probs.astype(jnp.bfloat16)).astype(jnp.float32)
    mixture = jnp.einsum("ghqk,gkhd->gqhd", probs_half, value_blocks) * inside
    attended = from_stretches(mixture.astype(jnp.bfloat16))
    layer_out = group_sum([(attended, out_weight)], N_MP).astype(jnp.bfloat16)

    d_attended = jnp.dot(grad_out, out_weight.T, preferred_element_type=jnp.float32).astype(jnp.bfloat16)
    out_grad = block_sum(attended, grad_out, SHARDS).astype(jnp.bfloat16)
    grad_blocks = to_stretches(d_attended, stretch_count) * inside
    grad_probs = jnp.einsum("gqhd,gkhd->ghqk", grad_blocks, value_blocks)
    value_terms = jnp.einsum("ghqk,gqhd->gkhd", probs_half, grad_blocks)
    grad_scores = soft_probs * (grad_probs - jnp.sum(soft_probs * grad_probs, -1, keepdims=True))
    scores_half = lax.optimization_barrier(grad_scores.astype(jnp.bfloat16)).astype(jnp.float32)
    query_terms = jnp.einsum("ghqk,gkhd->gqhd", scores_half, key_blocks) * score_scale
    key_terms = jnp.einsum("ghqk,gqhd->gkhd", scores_half, query_blocks) * score_scale
    grad_queries = from_stretches(query_terms.astype(jnp.bfloat16))
    grad_keys = key_terms.astype(jnp.bfloat16).reshape(NROWS, INNER)
    grad_values = value_terms.astype(jnp.bfloat16).reshape(NROWS, INNER)
    input_grad = group_sum([(grad_queries, query_weight.T)], N_MP).astype(jnp.bfloat16)
    query_grad = block_sum(tokens, grad_queries, SHARDS).astype(jnp.bfloat16)
    key_grad = jnp.dot(neighbours.T, grad_keys, preferred_element_type=jnp.float32).astype(jnp.bfloat16)
    value_grad = jnp.dot(neighbours.T, grad_values, preferred_element_type=jnp.float32).astype(jnp.bfloat16)
    row_grads = group_sum([(grad_keys, key_weight.T), (grad_values, value_weight.T)], N_MP).astype(jnp.bfloat16)
    encoding_grad = jnp.zeros((NROWS, ENC), jnp.bfloat16).at[source_rows].set(row_grads)
    return layer_out, input_grad, query_grad, key_grad, value_grad, out_grad, encoding_grad
```

```python
import jax
import jax.numpy as jnp
from jax import lax
from jax.experimental import pallas as pl
from jax.experimental.pallas import tpu as pltpu
from jax.sharding import PartitionSpec as P

HDIM = 128
ENC = 896
SHARD_ROWS = 28
PAD_ROWS = 32
SCALE = HDIM ** (-0.5)
BF = jnp.bfloat16
F32 = jnp.float32
N_SEMS = 256
MESH = pl.DeviceIdType.MESH


def dot(a, b, ca=1, cb=0):
    return lax.dot_general(a, b, (((ca,), (cb,)), ((), ())), preferred_element_type=F32)


def kernel(
    tok,
    gout,
    qw,
    ow,
    kw,
    vw,
    enc,
    place,
    omap,
    layer_out,
    input_grad,
    query_grad,
    pair_grad,
    out_grad,
    enc_grad,
    feats,
    gins,
    wall,
    spread,
    sorted_enc,
    earr,
    kvs,
    lp,
    ip,
    ep,
    rs1,
    rs1e,
    rs2,
    rs2e,
    mid,
    mide,
    tz,
    tzk,
    sib,
    sibk,
    uz,
    uzk,
    rodd,
    roddk,
    rch,
    rchk,
    chs,
    chsk,
    cbuf,
    crecv,
    eout,
    hall,
    send_sems,
    recv_sems,
    local_sems,
):
    d = lax.axis_index("dp")
    m = lax.axis_index("mp")
    z, c = d // 2, d % 2
    x, y = m // 4, m % 4

    def at(dz=0, dc=0, dx=0, dy=0):
        return (((z + dz + 16) % 16) * 2 + (c + dc) % 2, ((x + dx) % 4) * 4 + (y + dy) % 4)

    count = [0]
    sent = []

    def push(src, dst, to):
        i = count[0]
        count[0] += 1
        copy = pltpu.make_async_remote_copy(
            src_ref=src,
            dst_ref=dst,
            send_sem=send_sems.at[i],
            recv_sem=recv_sems.at[i],
            device_id=to,
            device_id_type=MESH,
        )
        copy.start()
        sent.append(copy)
        return copy

    low = (m - d + 32) % 16
    self_half = jnp.where(low == d % 16, d // 16, 2)

    barrier = pltpu.get_barrier_semaphore()
    after = ((d + 1) % 32, m)
    before = ((d + 31) % 32, m)
    peers = [at(dx=k) for k in (1, 2, 3)] + [at(dy=k) for k in (1, 2, 3)]
    peers += [at(dz=k) for k in (1, -1, 2, -2)] + [at(dc=1), after, before]
    for peer in peers:
        pl.semaphore_signal(barrier, inc=1, device_id=peer, device_id_type=MESH)
    for half in range(2):
        @pl.when(self_half != half)
        def _():
            pl.semaphore_signal(barrier, inc=1, device_id=(low + 16 * half, m), device_id_type=MESH)

    for h in range(2):
        feats[x, y, h] = tok[64 * h : 64 * h + 64, :]
        gins[x, y, h] = gout[64 * h : 64 * h + 64, :]
    wall[z, c, 0:64, :] = jnp.zeros((64, HDIM), BF)
    wall[z, c, 0:SHARD_ROWS, :] = kw[...]
    wall[z, c, PAD_ROWS : PAD_ROWS + SHARD_ROWS, :] = vw[...]
    wall[z, c, 64:192, :] = qw[...]
    wall[z, c, 192:320, :] = ow[...]
    pl.semaphore_wait(barrier, len(peers) + 2 - jnp.where(self_half < 2, 1, 0))

    def gather1(a):
        return [push(a.at[x, y, 0], a.at[x, y, 0], at(dx=k)) for k in (1, 3, 2)] + [
            push(a.at[x, y, 1], a.at[x, y, 1], at(dy=k)) for k in (1, 3, 2)
        ]

    def gather2(a, first):
        for copy in first:
            copy.wait_recv()
        return [push(a.at[:, y, 0], a.at[:, y, 0], at(dy=k)) for k in (1, 3, 2)] + [
            push(a.at[x, :, 1], a.at[x, :, 1], at(dx=k)) for k in (1, 3, 2)
        ]

    def landed(copies):
        for copy in copies:
            copy.wait_recv()

    pieces = ((0, 192), (192, 128))
    limits = ((8, 7), (7, 8))
    arriving = {}

    def forward(j):
        for p, (start, rows) in enumerate(pieces):
            for side, sign in enumerate((1, -1)):
                block = wall.at[(z - sign * 2 * j + 16) % 16, c, pl.ds(start, rows)]
                for step in (2, 1):
                    if 2 * j + step <= limits[p][side]:
                        arriving[p, side, 2 * j + step] = push(block, block, at(dz=sign * step))

    def to_sibling(dz):
        block = wall.at[(z + dz + 16) % 16, c]
        return push(block, block, at(dc=1))

    def wait_blocks(k):
        for p in range(2):
            for side in range(2):
                if k <= limits[p][side]:
                    arriving[p, side, k].wait_recv()

    siblings = []
    forward(0)
    f1 = gather1(feats)
    g1 = gather1(gins)

    rows_iota = lax.broadcasted_iota(jnp.int32, (512, 512), 0)
    spread[...] = jnp.where(rows_iota == place[...], 1.0, 0.0).astype(BF)
    sorted_enc[...] = dot(spread[...], enc[...], 0, 0).astype(BF)

    def relay(source, target, base):
        for half in range(2):
            peer = low + 16 * half
            copy = pltpu.make_async_remote_copy(
                src_ref=source(half, peer),
                dst_ref=target,
                send_sem=send_sems.at[base + half],
                recv_sem=recv_sems.at[base + d // 16],
                device_id=(peer, m),
                device_id_type=MESH,
            )
            local = pltpu.make_async_copy(
                source(half, peer), target, recv_sems.at[base + d // 16]
            )

            @pl.when(self_half == half)
            def _():
                local.start()

            @pl.when(self_half != half)
            def _():
                copy.start()

    def relay_landed(source, target, base):
        for half in range(2):
            copy = pltpu.make_async_remote_copy(
                src_ref=source(half, low),
                dst_ref=target(half),
                send_sem=send_sems.at[base + half],
                recv_sem=recv_sems.at[base + half],
                device_id=(low + 16 * half, m),
                device_id_type=MESH,
            )
            copy.wait_recv()

            @pl.when(self_half != half)
            def _():
                copy.wait_send()

    base_a = count[0]
    count[0] += 2

    def slot_block(half, peer):
        return sorted_enc.at[pl.ds(pl.multiple_of(peer * 16, 16), 16), :]

    relay(slot_block, earr.at[x, y, d // 16], base_a)
    siblings.append(to_sibling(0))

    wait_blocks(2)
    forward(1)
    f2 = gather2(feats, f1)
    g2 = gather2(gins, g1)
    relay_landed(slot_block, lambda half: earr.at[x, y, half], base_a)
    e1 = gather1(earr)
    siblings += [to_sibling(2), to_sibling(-2)]
    wait_blocks(4)
    forward(2)
    wait_blocks(1)
    siblings += [to_sibling(1), to_sibling(-1)]
    e2 = gather2(earr, e1)
    siblings += [to_sibling(4), to_sibling(-4)]
    wait_blocks(6)
    forward(3)
    siblings += [to_sibling(6), to_sibling(-6)]
    wait_blocks(3)
    siblings += [to_sibling(3), to_sibling(-3)]

    order = omap[...]
    source = order >> 4
    rank = (((source + d) & 15) << 5) + ((source >> 4) << 4) + (order & 15)
    spread_o = jnp.where(rows_iota == rank, 1.0, 0.0).astype(BF)

    wait_blocks(5)
    siblings += [to_sibling(5), to_sibling(-5)]
    wait_blocks(7)
    siblings += [to_sibling(7), to_sibling(-7)]
    wait_blocks(8)
    siblings.append(to_sibling(8))
    landed(siblings)
    landed(e2)

    e_iota = lax.broadcasted_iota(jnp.int32, (ENC, 1024), 0)
    p_iota = lax.broadcasted_iota(jnp.int32, (ENC, 1024), 1)
    within = p_iota & 31
    select = jnp.where(
        (within < SHARD_ROWS) & ((p_iota >> 5) * SHARD_ROWS + within == e_iota), 1.0, 0.0
    ).astype(BF)
    padded = jnp.concatenate(
        [
            wall[:, :, 0:32, :].reshape(1024, HDIM),
            wall[:, :, 32:64, :].reshape(1024, HDIM),
        ],
        1,
    )
    kv_weight = dot(select, padded).astype(BF)
    arrived = earr[...].reshape(512, ENC)
    kv_arrived = dot(arrived, kv_weight).astype(BF)
    kvs[256:768, :] = dot(spread_o, kv_arrived, 0, 0).astype(BF)
    shift = push(kvs.at[pl.ds(512, 256)], kvs.at[pl.ds(0, 256)], after)

    landed(f2)
    landed(g2)

    def block_of(a, i):
        return a[i // 4, i % 4].reshape(128, 256)

    def wq(i):
        return wall[i, :, 64:192, :].reshape(256, HDIM)

    def wo(i):
        return jnp.concatenate([wall[i, 0, 192:320, :], wall[i, 1, 192:320, :]], 1)

    queries = jnp.zeros((128, HDIM), F32)
    d_att = jnp.zeros((128, HDIM), F32)
    for i in range(16):
        queries += dot(block_of(feats, i), wq(i))
        d_att += dot(block_of(gins, i), wo(i), 1, 1)
    queries = queries.astype(BF)
    d_att = d_att.astype(BF)

    shift.wait_recv()
    keys = kvs[:, 0:HDIM]
    values = kvs[:, HDIM:]
    token = lax.broadcasted_iota(jnp.int32, (128, 768), 0)
    column = lax.broadcasted_iota(jnp.int32, (128, 768), 1)
    stretch = jnp.where(token >= 63, 1, 0) + jnp.where(token >= 127, 1, 0)
    first = jnp.where(d % 16 == 0, 1, 0)
    mask = ((column >> 8) == stretch) & (stretch >= first)
    scores = jnp.where(mask, dot(queries, keys, 1, 1) * SCALE, -1e30)
    top = jnp.max(scores, -1, keepdims=True)
    expo = jnp.where(mask, jnp.exp(scores - top), 0.0)
    total = jnp.sum(expo, -1, keepdims=True)
    probs = expo / jnp.where(total > 0.0, total, 1.0)
    probs_half = probs.astype(BF)
    attended = dot(probs_half, values).astype(BF)
    grad_probs = dot(d_att, values, 1, 1)
    grad_scores = (
        probs * (grad_probs - jnp.sum(probs * grad_probs, -1, keepdims=True))
    ).astype(BF)
    key_terms = dot(grad_scores, queries, 0, 0) * SCALE
    value_terms = dot(probs_half, d_att, 0, 0)
    pair_terms = jnp.concatenate([key_terms, value_terms], 1)
    cbuf[...] = pair_terms[0:256].astype(BF)
    carry = push(cbuf, crecv, before)
    grad_queries = (dot(grad_scores, keys) * SCALE).astype(BF)

    def scatter1(a, land):
        return [
            push(a.at[(x + k) % 4, :, 0], land.at[0, k - 1], at(dx=k)) for k in (1, 3, 2)
        ] + [push(a.at[:, (y + k) % 4, 1], land.at[1, k - 1], at(dy=k)) for k in (1, 3, 2)]

    def add_up(parts):
        total = parts[0].astype(F32)
        for part in parts[1:]:
            total = total + part.astype(F32)
        return total.astype(BF)

    def scatter2(a, land, half_sum, land2, first):
        landed(first)
        half_sum[0] = add_up([a[x, :, 0]] + [land[0, k] for k in range(3)])
        half_sum[1] = add_up([a[:, y, 1]] + [land[1, k] for k in range(3)])
        return [
            push(half_sum.at[0, (y + k) % 4], land2.at[0, k - 1], at(dy=k)) for k in (1, 3, 2)
        ] + [
            push(half_sum.at[1, (x + k) % 4], land2.at[1, k - 1], at(dx=k)) for k in (1, 3, 2)
        ]

    def scattered(half_sum, land2, second):
        landed(second)
        return [
            add_up([half_sum[0, y]] + [land2[0, k] for k in range(3)]),
            add_up([half_sum[1, x]] + [land2[1, k] for k in range(3)]),
        ]

    def z_swap(t, s):
        return push(t.at[:, 1 - c], s, at(dc=1))

    def z_odd(t, s, u, odd, chain, swap, sign):
        swap.wait_recv()
        for k in range(16):
            there = (z + sign * k + 16) % 16
            u[(k % 2) * 8 + k // 2] = add_up([t[there, c], s[there]])
        return [
            push(u.at[pl.ds(8, 4)], odd.at[0], at(dz=sign)),
            push(u.at[pl.ds(12, 4)], odd.at[1], at(dz=-sign)),
            push(u.at[4], chain.at[0, 3], at(dz=2 * sign)),
        ]

    def z_chain(u, odd, chain, out, before_, sign, j):
        landed(before_)
        ahead = [u[j], odd[0, j]]
        if j < 4:
            ahead.append(chain[0, j])
        behind = [u[8 - j], odd[1, 3 - j]]
        if j < 3:
            behind.append(chain[1, j])
        out[0, j] = add_up(ahead)
        out[1, j] = add_up(behind)
        return [
            push(out.at[0, j], chain.at[0, j - 1], at(dz=2 * sign)),
            push(out.at[1, j], chain.at[1, j - 1], at(dz=-2 * sign)),
        ]

    def z_end(u, odd, chain, before_):
        landed(before_)
        return add_up([u[0], odd[0, 0], odd[1, 3], chain[0, 0], chain[1, 0]])

    for i in range(16):
        part = dot(attended, wo(i)).astype(BF)
        lp[i // 4, i % 4] = part.reshape(2, 64, 256)
    lp1 = scatter1(lp, rs1.at[0])
    for i in range(16):
        part = dot(attended, block_of(gins, i), 0, 0).astype(BF)
        tz[0, i, 0] = part[:, 0:HDIM]
        tz[0, i, 1] = part[:, HDIM:]
    out_swap = z_swap(tz.at[0], sib.at[0])
    carry.wait_recv()
    pair_own = jnp.concatenate(
        [pair_terms[256:512], pair_terms[512:768] + crecv[...].astype(F32)], 0
    ).astype(BF)
    pair_arr = dot(spread_o, pair_own).astype(BF)
    ep[...] = dot(pair_arr, kv_weight, 1, 1).astype(BF).reshape(4, 4, 2, 16, ENC)
    ep1 = scatter1(ep, rs1e)
    for i in range(16):
        part = dot(grad_queries, wq(i), 1, 1).astype(BF)
        ip[i // 4, i % 4] = part.reshape(2, 64, 256)
    ip1 = scatter1(ip, rs1.at[1])
    for i in range(16):
        part = dot(block_of(feats, i), grad_queries, 0, 0).astype(BF)
        tz[1, i] = part.reshape(2, 128, HDIM)
    query_swap = z_swap(tz.at[1], sib.at[1])
    pair_part = dot(arrived, pair_arr, 0, 0).astype(BF)
    tzk[...] = dot(select, pair_part, 0, 0).astype(BF).reshape(16, 2, 32, 256)
    pair_swap = z_swap(tzk, sibk)

    zs = [
        (uz.at[0], rodd.at[0], rch.at[0], chs.at[0], 1),
        (uz.at[1], rodd.at[1], rch.at[1], chs.at[1], -1),
        (uzk, roddk, rchk, chsk, 1),
    ]
    steps = [
        z_odd(tz.at[0], sib.at[0], uz.at[0], rodd.at[0], rch.at[0], out_swap, 1),
        z_odd(tz.at[1], sib.at[1], uz.at[1], rodd.at[1], rch.at[1], query_swap, -1),
        z_odd(tzk, sibk, uzk, roddk, rchk, pair_swap, 1),
    ]

    def z_all(j):
        for i, (u, odd, chain, out, sign) in enumerate(zs):
            steps[i] = z_chain(u, odd, chain, out, steps[i], sign, j)

    lp2 = scatter2(lp, rs1.at[0], mid.at[0], rs2.at[0], lp1)
    z_all(3)
    ep2 = scatter2(ep, rs1e, mide, rs2e, ep1)
    ip2 = scatter2(ip, rs1.at[1], mid.at[1], rs2.at[1], ip1)
    halves = scattered(mid.at[0], rs2.at[0], lp2)
    for h in range(2):
        layer_out[x, y, h] = halves[h]
    lo1 = gather1(layer_out)
    z_all(2)
    halves = scattered(mide, rs2e, ep2)
    for h in range(2):
        eout[h] = halves[h]
    base_b = count[0]
    count[0] += 2
    relay(lambda half, peer: eout.at[half], hall.at[x, y, d // 16], base_b)
    halves = scattered(mid.at[1], rs2.at[1], ip2)
    for h in range(2):
        input_grad[64 * h : 64 * h + 64, :] = halves[h]
    z_all(1)
    lo2 = gather2(layer_out, lo1)
    relay_landed(lambda half, peer: eout.at[half], lambda half: hall.at[x, y, half], base_b)
    h1 = gather1(hall)
    out_grad[...] = z_end(uz.at[0], rodd.at[0], rch.at[0], steps[0])
    query_grad[...] = z_end(uz.at[1], rodd.at[1], rch.at[1], steps[1])
    pair_grad[...] = z_end(uzk, roddk, rchk, steps[2])
    h2 = gather2(hall, h1)
    landed(lo2)
    landed(h2)
    for i in range(16):
        for half in range(2):
            owner = (i - d + 32) % 16 + 16 * half
            sorted_enc[pl.ds(pl.multiple_of(owner * 16, 16), 16), :] = hall[i // 4, i % 4, half]
    enc_grad[...] = dot(spread[...], sorted_enc[...]).astype(BF)
    for copy in sent:
        copy.wait_send()


def shards(
    tokens,
    encodings,
    shard_place,
    owner_map,
    query_weight,
    key_weight,
    value_weight,
    out_weight,
    grad_out,
):
    vmem = pl.BlockSpec(memory_space=pltpu.VMEM)
    outs = [
        jax.ShapeDtypeStruct((4, 4, 2, 64, 256), BF),
        jax.ShapeDtypeStruct((128, 256), BF),
        jax.ShapeDtypeStruct((128, 128), BF),
        jax.ShapeDtypeStruct((32, 256), BF),
        jax.ShapeDtypeStruct((128, 128), BF),
        jax.ShapeDtypeStruct((512, ENC), BF),
    ]
    shapes = [
        (4, 4, 2, 64, 256),
        (4, 4, 2, 64, 256),
        (16, 2, 320, 128),
        (512, 512),
        (512, ENC),
        (4, 4, 2, 16, ENC),
        (768, 256),
        (4, 4, 2, 64, 256),
        (4, 4, 2, 64, 256),
        (4, 4, 2, 16, ENC),
        (2, 2, 3, 4, 64, 256),
        (2, 3, 4, 16, ENC),
        (2, 2, 3, 64, 256),
        (2, 3, 16, ENC),
        (2, 2, 4, 64, 256),
        (2, 4, 16, ENC),
        (2, 16, 2, 128, 128),
        (16, 2, 32, 256),
        (2, 16, 128, 128),
        (16, 32, 256),
        (2, 16, 128, 128),
        (16, 32, 256),
        (2, 2, 4, 128, 128),
        (2, 4, 32, 256),
        (2, 2, 4, 128, 128),
        (2, 4, 32, 256),
        (2, 2, 4, 128, 128),
        (2, 4, 32, 256),
        (256, 256),
        (256, 256),
        (2, 16, ENC),
        (4, 4, 2, 16, ENC),
    ]
    scratch = [pltpu.VMEM(shape, BF) for shape in shapes]
    scratch += [
        pltpu.SemaphoreType.DMA((N_SEMS,)),
        pltpu.SemaphoreType.DMA((N_SEMS,)),
        pltpu.SemaphoreType.DMA((8,)),
    ]
    layer, input_grad, query_grad, pair_grad, out_grad, enc_grad = pl.pallas_call(
        kernel,
        out_shape=outs,
        in_specs=[vmem] * 9,
        out_specs=[vmem] * 6,
        scratch_shapes=scratch,
        compiler_params=pltpu.CompilerParams(
            collective_id=0, has_side_effects=True, vmem_limit_bytes=56 * 1024 * 1024
        ),
        name="retro",
    )(
        tokens,
        grad_out,
        query_weight,
        out_weight,
        key_weight,
        value_weight,
        encodings,
        shard_place,
        owner_map,
    )
    layer_out = layer.reshape(16, 128, 256).transpose(1, 0, 2).reshape(128, 4096)
    key_grad = pair_grad[:SHARD_ROWS, :HDIM]
    value_grad = pair_grad[:SHARD_ROWS, HDIM:]
    return (layer_out, input_grad, query_grad, key_grad, value_grad, out_grad, enc_grad)


def solution(mesh):
    placed = (
        P("dp", "mp"),
        P("dp", None),
        P("dp", None),
        P("dp", None),
        P("dp", "mp"),
        P("dp", "mp"),
        P("dp", "mp"),
        P("mp", "dp"),
        P("dp", "mp"),
    )
    return jax.shard_map(
        shards,
        mesh=mesh,
        in_specs=placed,
        out_specs=(
            P("dp", None),
            P("dp", "mp"),
            P("dp", "mp"),
            P("dp", "mp"),
            P("dp", "mp"),
            P("mp", "dp"),
            P("dp", None),
        ),
        check_vma=False,
    )
```

```python
import jax
import jax.numpy as jnp
from jax import lax
from jax.experimental import pallas as pl
from jax.experimental.pallas import tpu as pltpu
from jax.sharding import PartitionSpec as P

HDIM = 128
ENC = 896
SHARD_ROWS = 28
PAD_ROWS = 32
SCALE = HDIM ** (-0.5)
BF = jnp.bfloat16
F32 = jnp.float32
N_SEMS = 113
MESH = pl.DeviceIdType.MESH


def dot(a, b, ca=1, cb=0):
    return lax.dot_general(a, b, (((ca,), (cb,)), ((), ())), preferred_element_type=F32)


def kernel(
    tok,
    gout,
    qw,
    ow,
    kw,
    vw,
    enc,
    place,
    omap,
    layer_hbm,
    input_hbm,
    query_hbm,
    pair_hbm,
    out_hbm,
    enc_hbm,
    encs,
    flat,
    layer_out,
    input_grad,
    query_grad,
    pair_grad,
    out_grad,
    enc_grad,
    feats,
    gins,
    wall,
    spread,
    sorted_enc,
    relayed,
    earr,
    kvs,
    lp,
    ip,
    ep,
    rs1,
    rs1e,
    rs2,
    rs2e,
    mid,
    mide,
    tz,
    tzk,
    sib,
    sibk,
    uz,
    uzk,
    rodd,
    roddk,
    rch,
    rchk,
    chs,
    chsk,
    cbuf,
    crecv,
    eout,
    hall,
    many,
    many_e,
    sems,
    local_sems,
):
    d = lax.axis_index("dp")
    m = lax.axis_index("mp")
    z, c = d // 2, d % 2
    x, y = m // 4, m % 4

    def at(dz=0, dc=0, dx=0, dy=0):
        return (((z + dz + 16) % 16) * 2 + (c + dc) % 2, ((x + dx) % 4) * 4 + (y + dy) % 4)

    count = [0]
    finals = []

    def sem():
        count[0] += 1
        return sems.at[count[0] - 1]

    def push(src, dst, to, send, recv):
        pltpu.make_async_remote_copy(
            src_ref=src,
            dst_ref=dst,
            send_sem=send,
            recv_sem=recv,
            device_id=to,
            device_id_type=MESH,
        ).start()

    def drain(ref, one):
        pltpu.make_async_copy(ref, ref, one).wait()

    low = (m - d + 32) % 16
    self_half = jnp.where(low == d % 16, d // 16, 2)

    barrier = pltpu.get_barrier_semaphore()
    after = ((d + 1) % 32, m)
    before = ((d + 31) % 32, m)
    peers = [at(dx=k) for k in (1, 2, 3)] + [at(dy=k) for k in (1, 2, 3)]
    peers += [at(dz=k) for k in (1, -1, 2, -2)] + [at(dc=1), after, before]
    for peer in peers:
        pl.semaphore_signal(barrier, inc=1, device_id=peer, device_id_type=MESH)
    for half in range(2):
        @pl.when(self_half != half)
        def _():
            pl.semaphore_signal(barrier, inc=1, device_id=(low + 16 * half, m), device_id_type=MESH)

    loads = [
        (enc, encs),
        (qw, wall.at[z, c, pl.ds(64, 128)]),
        (ow, wall.at[z, c, pl.ds(192, 128)]),
    ]
    for h in range(2):
        loads.append((tok.at[pl.ds(64 * h, 64)], feats.at[x, y, h]))
        loads.append((gout.at[pl.ds(64 * h, 64)], gins.at[x, y, h]))
    loads = [
        pltpu.make_async_copy(src, dst, local_sems.at[i]) for i, (src, dst) in enumerate(loads)
    ]
    for load in loads:
        load.start()
    wall[z, c, 0:64, :] = jnp.zeros((64, HDIM), BF)
    wall[z, c, 0:SHARD_ROWS, :] = kw[...]
    wall[z, c, PAD_ROWS : PAD_ROWS + SHARD_ROWS, :] = vw[...]

    rows_iota = lax.broadcasted_iota(jnp.int32, (512, 512), 0)
    spread[...] = jnp.where(rows_iota == place[...], 1.0, 0.0).astype(BF)
    loads[0].wait()
    r_iota = lax.broadcasted_iota(jnp.int32, (32, 512), 0)
    s_iota = lax.broadcasted_iota(jnp.int32, (32, 512), 1)
    picked = low * 16 + r_iota + jnp.where(r_iota >= 16, 240, 0)
    pick = jnp.where(s_iota == picked, 1.0, 0.0).astype(BF)
    chosen = dot(pick, spread[...], 1, 1).astype(BF)
    relayed[...] = dot(chosen, encs[...]).astype(BF).reshape(2, 16, ENC)
    for load in loads[1:]:
        load.wait()
    stores = []

    def store(src, dst):
        copy = pltpu.make_async_copy(src, dst, local_sems.at[8 + len(stores)])
        copy.start()
        stores.append(copy)

    pl.semaphore_wait(barrier, len(peers) + 2 - jnp.where(self_half < 2, 1, 0))

    def gather1(a, wide):
        send, rest = sem(), sem()
        finals.append((wide, send))
        ahead = [sem() for _ in range(3)]
        across = [sem() for _ in range(3)]
        block0, block1 = a.at[x, y, 0], a.at[x, y, 1]
        for i, k in enumerate((1, 3, 2)):
            push(block0, block0, at(dx=k), send, ahead[i])
            push(block1, block1, at(dy=k), send, across[i])
        for k in (1, 3, 2):
            push(block0, block0, at(dy=k), send, rest)
            push(block1, block1, at(dx=k), send, rest)
        return send, rest, ahead, across

    def gather2(a, first):
        send, rest, ahead, across = first
        for i, k in enumerate((1, 3, 2)):
            block = a.at[(x + 4 - k) % 4, y, 0]
            drain(block, ahead[i])
            for j in (1, 3, 2):
                push(block, block, at(dy=j), send, rest)
            block = a.at[x, (y + 4 - k) % 4, 1]
            drain(block, across[i])
            for j in (1, 3, 2):
                push(block, block, at(dx=j), send, rest)
        return a.at[pl.ds(0, 3)], rest

    def landed(end):
        drain(*end)

    pieces = ((0, 64), (64, 128), (192, 128))
    limits = ((8, 7), (7, 8), (8, 7))
    arriving = [{k: sem() for k in range(1, 9)} for _ in pieces]
    sending = [sem() for _ in pieces]
    for (start, rows), one in zip(pieces, sending):
        finals.append((wall.at[pl.ds(0, 15), 0, pl.ds(start, rows)], one))

    def forward(p, j):
        start, rows = pieces[p]
        for step in (2, 1):
            k = 2 * j + step
            for side, sign in enumerate((1, -1)):
                if k <= limits[p][side]:
                    block = wall.at[(z - sign * 2 * j + 16) % 16, c, pl.ds(start, rows)]
                    push(block, block, at(dz=sign * step), sending[p], arriving[p][k])

    crossing = {0: (sem(), sem()), 64: (sem(), sem())}
    for start, rows in ((0, 64), (64, 256)):
        finals.append((wall.at[:, 0, pl.ds(start, rows)], crossing[start][0]))

    def to_sibling(dz, start, rows):
        block = wall.at[(z + dz + 16) % 16, c, pl.ds(start, rows)]
        push(block, block, at(dc=1), *crossing[start])

    def all_crossed(start, rows):
        drain(wall.at[:, 0, pl.ds(start, rows)], crossing[start][1])

    def wait_blocks(p, k):
        start, rows = pieces[p]
        drain(wall.at[pl.ds(0, len(both(k))), 0, pl.ds(start, rows)], arriving[p][k])

    def both(k):
        return (k, -k) if k < 8 else (8,)

    def relay(source, target, pair):
        sends, recvs = pair
        for half in range(2):
            peer = low + 16 * half

            @pl.when(self_half == half)
            def _():
                pltpu.make_async_copy(source.at[half], target, recvs.at[d // 16]).start()

            @pl.when(self_half != half)
            def _():
                push(source.at[half], target, (peer, m), sends.at[half], recvs.at[d // 16])

    def relay_landed(source, target, pair):
        sends, recvs = pair
        for half in range(2):
            drain(target(half), recvs.at[half])

            @pl.when(self_half != half)
            def _():
                drain(source.at[half], sends.at[half])

    def two():
        count[0] += 2
        return sems.at[pl.ds(count[0] - 2, 2)]

    pair_a = two(), two()
    relay(relayed, earr.at[x, y, d // 16], pair_a)
    forward(0, 0)
    f1 = gather1(feats, many)
    forward(1, 0)
    g1 = gather1(gins, many)
    forward(2, 0)
    to_sibling(0, 0, 64)
    to_sibling(0, 64, 256)
    order = omap[...]
    source = order >> 4
    rank = (((source + d) & 15) << 5) + ((source >> 4) << 4) + (order & 15)
    spread_o = jnp.where(rows_iota == rank, 1.0, 0.0).astype(BF)

    e_iota = lax.broadcasted_iota(jnp.int32, (ENC, 1024), 0)
    p_iota = lax.broadcasted_iota(jnp.int32, (ENC, 1024), 1)
    within = p_iota & 31
    select = jnp.where(
        (within < SHARD_ROWS) & ((p_iota >> 5) * SHARD_ROWS + within == e_iota), 1.0, 0.0
    ).astype(BF)

    for p in range(3):
        wait_blocks(p, 2)
        forward(p, 1)
    relay_landed(relayed, lambda half: earr.at[x, y, half], pair_a)
    e1 = gather1(earr, many_e)
    for i in both(2):
        to_sibling(i, 0, 64)
    for i in both(2):
        to_sibling(i, 64, 256)
    f2 = gather2(feats, f1)
    for p in range(3):
        wait_blocks(p, 4)
        forward(p, 2)
    e2 = gather2(earr, e1)
    g2 = gather2(gins, g1)
    for i in both(4):
        to_sibling(i, 0, 64)
    for i in both(4):
        to_sibling(i, 64, 256)
    for k in (1, 3):
        wait_blocks(0, k)
        for i in both(k):
            to_sibling(i, 0, 64)
    for p in range(3):
        wait_blocks(p, 6)
        forward(p, 3)
    for i in both(6):
        to_sibling(i, 0, 64)
    for i in both(6):
        to_sibling(i, 64, 256)
    for k in (1, 3):
        wait_blocks(1, k)
        wait_blocks(2, k)
        for i in both(k):
            to_sibling(i, 64, 256)
    for k in (5, 7, 8):
        wait_blocks(0, k)
        for i in both(k):
            to_sibling(i, 0, 64)
    all_crossed(0, 64)
    landed(e2)

    padded = jnp.concatenate(
        [
            wall[:, :, 0:32, :].reshape(1024, HDIM),
            wall[:, :, 32:64, :].reshape(1024, HDIM),
        ],
        1,
    )
    kv_weight = dot(select, padded).astype(BF)
    arrived = earr[...].reshape(512, ENC)
    kv_arrived = dot(arrived, kv_weight).astype(BF)
    kvs[256:768, :] = dot(spread_o, kv_arrived, 0, 0).astype(BF)
    shift = sem(), sem()
    finals.append((kvs.at[pl.ds(0, 256)], shift[0]))
    push(kvs.at[pl.ds(512, 256)], kvs.at[pl.ds(0, 256)], after, *shift)

    landed(f2)
    landed(g2)

    def block_of(a, i):
        return a[i // 4, i % 4].reshape(128, 256)

    def wq(i):
        return wall[i, :, 64:192, :].reshape(256, HDIM)

    def wo(i):
        return jnp.concatenate([wall[i, 0, 192:320, :], wall[i, 1, 192:320, :]], 1)

    queries = jnp.zeros((128, HDIM), F32)
    d_att = jnp.zeros((128, HDIM), F32)
    for k in (0, 2, 4, 6, 1, 3, 5, 7, 8):
        if k in (5, 7, 8):
            wait_blocks(1, k)
            wait_blocks(2, k)
            for i in both(k):
                to_sibling(i, 64, 256)
    all_crossed(64, 256)
    for k in (0, 2, 4, 6, 1, 3, 5, 7, 8):
        for dz in (0,) if k == 0 else both(k):
            i = (z + dz + 16) % 16
            queries += dot(block_of(feats, i), wq(i))
            d_att += dot(block_of(gins, i), wo(i), 1, 1)
    queries = queries.astype(BF)
    d_att = d_att.astype(BF)

    drain(kvs.at[pl.ds(0, 256)], shift[1])
    keys = kvs[:, 0:HDIM]
    values = kvs[:, HDIM:]
    token = lax.broadcasted_iota(jnp.int32, (128, 768), 0)
    column = lax.broadcasted_iota(jnp.int32, (128, 768), 1)
    stretch = jnp.where(token >= 63, 1, 0) + jnp.where(token >= 127, 1, 0)
    first = jnp.where(d % 16 == 0, 1, 0)
    mask = ((column >> 8) == stretch) & (stretch >= first)
    scores = jnp.where(mask, dot(queries, keys, 1, 1) * SCALE, -1e30)
    top = jnp.max(scores, -1, keepdims=True)
    expo = jnp.where(mask, jnp.exp(scores - top), 0.0)
    total = jnp.sum(expo, -1, keepdims=True)
    probs = expo / jnp.where(total > 0.0, total, 1.0)
    probs_half = probs.astype(BF)
    attended = dot(probs_half, values).astype(BF)
    grad_probs = dot(d_att, values, 1, 1)
    grad_scores = (
        probs * (grad_probs - jnp.sum(probs * grad_probs, -1, keepdims=True))
    ).astype(BF)
    key_terms = dot(grad_scores, queries, 0, 0) * SCALE
    value_terms = dot(probs_half, d_att, 0, 0)
    pair_terms = jnp.concatenate([key_terms, value_terms], 1)
    cbuf[...] = pair_terms[0:256].astype(BF)
    carry = sem(), sem()
    finals.append((cbuf, carry[0]))
    push(cbuf, crecv, before, *carry)
    grad_queries = (dot(grad_scores, keys) * SCALE).astype(BF)

    def scatter1(a, land, wide):
        send, recv = sem(), sem()
        finals.append((wide, send))
        for k in (1, 3, 2):
            push(a.at[(x + k) % 4, :, 0], land.at[0, k - 1], at(dx=k), send, recv)
            push(a.at[:, (y + k) % 4, 1], land.at[1, k - 1], at(dy=k), send, recv)
        return send, recv

    def add_up(parts):
        total = parts[0].astype(F32)
        for part in parts[1:]:
            total = total + part.astype(F32)
        return total.astype(BF)

    def scatter2(a, land, half_sum, land2, first):
        send, recv = first
        drain(land, recv)
        half_sum[0] = add_up([a[x, :, 0]] + [land[0, k] for k in range(3)])
        half_sum[1] = add_up([a[:, y, 1]] + [land[1, k] for k in range(3)])
        recv = sem()
        for k in (1, 3, 2):
            push(half_sum.at[0, (y + k) % 4], land2.at[0, k - 1], at(dy=k), send, recv)
            push(half_sum.at[1, (x + k) % 4], land2.at[1, k - 1], at(dx=k), send, recv)
        return recv

    def scattered(half_sum, land2, recv):
        drain(land2, recv)
        return [
            add_up([half_sum[0, y]] + [land2[0, k] for k in range(3)]),
            add_up([half_sum[1, x]] + [land2[1, k] for k in range(3)]),
        ]

    def z_swap(t, s):
        send, recv = sem(), sem()
        finals.append((s, send))
        push(t.at[:, 1 - c], s, at(dc=1), send, recv)
        return recv

    def z_odd(t, s, u, odd, chain, swap, sign):
        drain(s, swap)
        for k in range(16):
            there = (z + sign * k + 16) % 16
            u[(k % 2) * 8 + k // 2] = add_up([t[there, c], s[there]])
        send, recv = sem(), sem()
        finals.append((u.at[pl.ds(0, 15)], send))
        push(u.at[4], chain.at[0, 3], at(dz=2 * sign), send, recv)
        push(u.at[pl.ds(8, 4)], odd.at[0], at(dz=sign), send, recv)
        push(u.at[pl.ds(12, 4)], odd.at[1], at(dz=-sign), send, recv)
        return send, recv, u.at[pl.ds(0, 9)]

    def z_chain(u, odd, chain, out, step, sign, j):
        send, recv, size = step
        drain(size, recv)
        ahead = [u[j], odd[0, j], chain[0, j]]
        behind = [u[8 - j], odd[1, 3 - j]]
        if j < 3:
            behind.append(chain[1, j])
        out[0, j] = add_up(ahead)
        out[1, j] = add_up(behind)
        recv = sem()
        push(out.at[0, j], chain.at[0, j - 1], at(dz=2 * sign), send, recv)
        push(out.at[1, j], chain.at[1, j - 1], at(dz=-2 * sign), send, recv)
        return send, recv, u.at[pl.ds(0, 2)]

    def z_end(u, odd, chain, step):
        drain(step[2], step[1])
        return add_up([u[0], odd[0, 0], odd[1, 3], chain[0, 0], chain[1, 0]])

    for i in range(16):
        part = dot(attended, wo(i)).astype(BF)
        lp[i // 4, i % 4] = part.reshape(2, 64, 256)
    lp1 = scatter1(lp, rs1.at[0], many)
    for i in range(16):
        part = dot(attended, block_of(gins, i), 0, 0).astype(BF)
        tz[0, i, 0] = part[:, 0:HDIM]
        tz[0, i, 1] = part[:, HDIM:]
    out_swap = z_swap(tz.at[0], sib.at[0])
    drain(crecv, carry[1])
    pair_own = jnp.concatenate(
        [pair_terms[256:512], pair_terms[512:768] + crecv[...].astype(F32)], 0
    ).astype(BF)
    pair_arr = dot(spread_o, pair_own).astype(BF)
    ep[...] = dot(pair_arr, kv_weight, 1, 1).astype(BF).reshape(4, 4, 2, 16, ENC)
    ep1 = scatter1(ep, rs1e, many_e)
    for i in range(16):
        part = dot(grad_queries, wq(i), 1, 1).astype(BF)
        ip[i // 4, i % 4] = part.reshape(2, 64, 256)
    ip1 = scatter1(ip, rs1.at[1], many)
    for i in range(16):
        part = dot(block_of(feats, i), grad_queries, 0, 0).astype(BF)
        tz[1, i] = part.reshape(2, 128, HDIM)
    query_swap = z_swap(tz.at[1], sib.at[1])
    pair_part = dot(arrived, pair_arr, 0, 0).astype(BF)
    tzk[...] = dot(select, pair_part, 0, 0).astype(BF).reshape(16, 2, 32, 256)
    pair_swap = z_swap(tzk, sibk)

    zs = [
        (uz.at[0], rodd.at[0], rch.at[0], chs.at[0], 1),
        (uz.at[1], rodd.at[1], rch.at[1], chs.at[1], -1),
        (uzk, roddk, rchk, chsk, 1),
    ]
    steps = [
        z_odd(tz.at[0], sib.at[0], uz.at[0], rodd.at[0], rch.at[0], out_swap, 1),
        z_odd(tz.at[1], sib.at[1], uz.at[1], rodd.at[1], rch.at[1], query_swap, -1),
        z_odd(tzk, sibk, uzk, roddk, rchk, pair_swap, 1),
    ]

    def z_all(j):
        for i, (u, odd, chain, out, sign) in enumerate(zs):
            steps[i] = z_chain(u, odd, chain, out, steps[i], sign, j)

    lp2 = scatter2(lp, rs1.at[0], mid.at[0], rs2.at[0], lp1)
    ep2 = scatter2(ep, rs1e, mide, rs2e, ep1)
    z_all(3)
    halves = scattered(mid.at[0], rs2.at[0], lp2)
    for h in range(2):
        layer_out[x, y, h] = halves[h]
    lo1 = gather1(layer_out, many)
    halves = scattered(mide, rs2e, ep2)
    for h in range(2):
        eout[h] = halves[h]
    pair_b = two(), two()
    relay(eout, hall.at[x, y, d // 16], pair_b)
    ip2 = scatter2(ip, rs1.at[1], mid.at[1], rs2.at[1], ip1)
    z_all(2)
    lo2 = gather2(layer_out, lo1)
    relay_landed(eout, lambda half: hall.at[x, y, half], pair_b)
    h1 = gather1(hall, many_e)
    z_all(1)
    halves = scattered(mid.at[1], rs2.at[1], ip2)
    for h in range(2):
        input_grad[64 * h : 64 * h + 64, :] = halves[h]
    store(input_grad, input_hbm)
    h2 = gather2(hall, h1)
    out_grad[...] = z_end(uz.at[0], rodd.at[0], rch.at[0], steps[0])
    store(out_grad, out_hbm)
    query_grad[...] = z_end(uz.at[1], rodd.at[1], rch.at[1], steps[1])
    store(query_grad, query_hbm)
    pair_grad[...] = z_end(uzk, roddk, rchk, steps[2])
    store(pair_grad, pair_hbm)
    landed(lo2)
    for i in range(16):
        flat[:, 256 * i : 256 * i + 256] = block_of(layer_out, i)
    store(flat, layer_hbm)
    landed(h2)
    for i in range(16):
        for half in range(2):
            owner = (i - d + 32) % 16 + 16 * half
            sorted_enc[pl.ds(pl.multiple_of(owner * 16, 16), 16), :] = hall[i // 4, i % 4, half]
    enc_grad[...] = dot(spread[...], sorted_enc[...]).astype(BF)
    store(enc_grad, enc_hbm)
    for copy in stores:
        copy.wait()
    for end in finals:
        drain(*end)
    assert count[0] == N_SEMS, count[0]


def finish(
    layer, input_g, query_g, pair_g, out_g, enc_g,
    layer_out, input_out, query_out, key_out, value_out, out_out, enc_out,
    held_l, held_i, held_q, held_p, held_o, held_e, sems,
):
    pairs = [
        (layer, held_l, layer_out),
        (enc_g, held_e, enc_out),
        (input_g, held_i, input_out),
        (query_g, held_q, query_out),
        (out_g, held_o, out_out),
    ]
    ins = [
        pltpu.make_async_copy(src, held, sems.at[i]) for i, (src, held, _) in enumerate(pairs)
    ]
    outs = [
        pltpu.make_async_copy(held, dst, sems.at[8 + i])
        for i, (_, held, dst) in enumerate(pairs)
    ]
    pair_in = pltpu.make_async_copy(pair_g, held_p, sems.at[7])
    pair_in.start()
    for copy in ins:
        copy.start()
    pair_in.wait()
    key_out[...] = held_p[0:SHARD_ROWS, 0:HDIM]
    value_out[...] = held_p[0:SHARD_ROWS, HDIM:]
    for copy, onward in zip(ins, outs):
        copy.wait()
        onward.start()
    for copy in outs:
        copy.wait()


def shards(
    tokens,
    encodings,
    shard_place,
    owner_map,
    query_weight,
    key_weight,
    value_weight,
    out_weight,
    grad_out,
):
    vmem = pl.BlockSpec(memory_space=pltpu.VMEM)
    hbm = pl.BlockSpec(memory_space=pl.ANY)
    outs = [
        jax.ShapeDtypeStruct((128, 4096), BF),
        jax.ShapeDtypeStruct((128, 256), BF),
        jax.ShapeDtypeStruct((128, 128), BF),
        jax.ShapeDtypeStruct((32, 256), BF),
        jax.ShapeDtypeStruct((128, 128), BF),
        jax.ShapeDtypeStruct((512, ENC), BF),
    ]
    shapes = [
        (512, ENC),
        (128, 4096),
        (4, 4, 2, 64, 256),
        (128, 256),
        (128, 128),
        (32, 256),
        (128, 128),
        (512, ENC),
        (4, 4, 2, 64, 256),
        (4, 4, 2, 64, 256),
        (16, 2, 320, 128),
        (512, 512),
        (512, ENC),
        (2, 16, ENC),
        (4, 4, 2, 16, ENC),
        (768, 256),
        (4, 4, 2, 64, 256),
        (4, 4, 2, 64, 256),
        (4, 4, 2, 16, ENC),
        (2, 2, 3, 4, 64, 256),
        (2, 3, 4, 16, ENC),
        (2, 2, 3, 64, 256),
        (2, 3, 16, ENC),
        (2, 2, 4, 64, 256),
        (2, 4, 16, ENC),
        (2, 16, 2, 128, 128),
        (16, 2, 32, 256),
        (2, 16, 128, 128),
        (16, 32, 256),
        (2, 16, 128, 128),
        (16, 32, 256),
        (2, 2, 4, 128, 128),
        (2, 4, 32, 256),
        (2, 2, 4, 128, 128),
        (2, 4, 32, 256),
        (2, 2, 4, 128, 128),
        (2, 4, 32, 256),
        (256, 256),
        (256, 256),
        (2, 16, ENC),
        (4, 4, 2, 16, ENC),
        (30, 64, 256),
        (30, 16, ENC),
    ]
    scratch = [pltpu.VMEM(shape, BF) for shape in shapes]
    scratch += [
        pltpu.SemaphoreType.DMA((N_SEMS,)),
        pltpu.SemaphoreType.DMA((14,)),
    ]
    parts = pl.pallas_call(
        kernel,
        out_shape=outs,
        in_specs=[hbm] * 4 + [vmem] * 2 + [hbm] + [vmem] * 2,
        out_specs=[hbm] * 6,
        scratch_shapes=scratch,
        compiler_params=pltpu.CompilerParams(
            collective_id=0, has_side_effects=True, vmem_limit_bytes=56 * 1024 * 1024
        ),
        name="retro",
    )(
        tokens,
        grad_out,
        query_weight,
        out_weight,
        key_weight,
        value_weight,
        encodings,
        shard_place,
        owner_map,
    )
    shapes = [
        (128, 4096),
        (128, 256),
        (128, 128),
        (SHARD_ROWS, 128),
        (SHARD_ROWS, 128),
        (128, 128),
        (512, ENC),
    ]
    return pl.pallas_call(
        finish,
        out_shape=[jax.ShapeDtypeStruct(shape, BF) for shape in shapes],
        in_specs=[hbm] * 6,
        out_specs=[hbm] * 3 + [vmem] * 2 + [hbm] * 2,
        scratch_shapes=[
            pltpu.VMEM((128, 4096), BF),
            pltpu.VMEM((128, 256), BF),
            pltpu.VMEM((128, 128), BF),
            pltpu.VMEM((32, 256), BF),
            pltpu.VMEM((128, 128), BF),
            pltpu.VMEM((512, ENC), BF),
            pltpu.SemaphoreType.DMA((16,)),
        ],
        name="finish",
    )(*parts)


def solution(mesh):
    placed = (
        P("dp", "mp"),
        P("dp", None),
        P("dp", None),
        P("dp", None),
        P("dp", "mp"),
        P("dp", "mp"),
        P("dp", "mp"),
        P("mp", "dp"),
        P("dp", "mp"),
    )
    return jax.shard_map(
        shards,
        mesh=mesh,
        in_specs=placed,
        out_specs=(
            P("dp", None),
            P("dp", "mp"),
            P("dp", "mp"),
            P("dp", "mp"),
            P("dp", "mp"),
            P("mp", "dp"),
            P("dp", None),
        ),
        check_vma=False,
    )
```

```python
import jax
import jax.numpy as jnp
from jax import lax
from jax.experimental import pallas as pl
from jax.experimental.pallas import tpu as pltpu
from jax.sharding import PartitionSpec as P

HDIM = 128
ENC = 896
SHARD_ROWS = 28
PAD_ROWS = 32
SCALE = HDIM ** (-0.5)
BF = jnp.bfloat16
F32 = jnp.float32
N_SEMS = 115
MESH = pl.DeviceIdType.MESH


def dot(a, b, ca=1, cb=0):
    return lax.dot_general(a, b, (((ca,), (cb,)), ((), ())), preferred_element_type=F32)


def kernel(
    tok,
    gout,
    qw,
    ow,
    kw,
    vw,
    enc,
    place,
    omap,
    layer_hbm,
    input_hbm,
    query_hbm,
    pair_hbm,
    out_hbm,
    enc_hbm,
    encs,
    flat,
    layer_out,
    input_grad,
    query_grad,
    pair_grad,
    out_grad,
    enc_grad,
    feats,
    gins,
    wall,
    spread,
    sorted_enc,
    relayed,
    earr,
    kvs,
    lp,
    ip,
    ep,
    rs1,
    rs1e,
    rs2,
    rs2e,
    mid,
    mide,
    tz,
    tzk,
    sib,
    sibk,
    uz,
    uzk,
    rodd,
    roddk,
    rch,
    rchk,
    chs,
    chsk,
    cbuf,
    crecv,
    eout,
    hall,
    many,
    many_e,
    sems,
    local_sems,
):
    d = lax.axis_index("dp")
    m = lax.axis_index("mp")
    z, c = d // 2, d % 2
    x, y = m // 4, m % 4

    def at(dz=0, dc=0, dx=0, dy=0):
        return (((z + dz + 16) % 16) * 2 + (c + dc) % 2, ((x + dx) % 4) * 4 + (y + dy) % 4)

    count = [0]
    finals = []

    def sem():
        count[0] += 1
        return sems.at[count[0] - 1]

    def push(src, dst, to, send, recv):
        pltpu.make_async_remote_copy(
            src_ref=src,
            dst_ref=dst,
            send_sem=send,
            recv_sem=recv,
            device_id=to,
            device_id_type=MESH,
        ).start()

    def drain(ref, one):
        pltpu.make_async_copy(ref, ref, one).wait()

    low = (m - d + 32) % 16
    self_half = jnp.where(low == d % 16, d // 16, 2)

    barrier = pltpu.get_barrier_semaphore()
    after = ((d + 1) % 32, m)
    before = ((d + 31) % 32, m)
    peers = [at(dx=k) for k in (1, 2, 3)] + [at(dy=k) for k in (1, 2, 3)]
    peers += [at(dz=k) for k in (1, -1, 2, -2)] + [at(dc=1), after, before]
    for peer in peers:
        pl.semaphore_signal(barrier, inc=1, device_id=peer, device_id_type=MESH)
    for half in range(2):
        @pl.when(self_half != half)
        def _():
            pl.semaphore_signal(barrier, inc=1, device_id=(low + 16 * half, m), device_id_type=MESH)

    loads = [
        (enc, encs),
        (qw, wall.at[z, c, pl.ds(64, 128)]),
        (ow, wall.at[z, c, pl.ds(192, 128)]),
    ]
    for h in range(2):
        loads.append((tok.at[pl.ds(64 * h, 64)], feats.at[x, y, h]))
        loads.append((gout.at[pl.ds(64 * h, 64)], gins.at[x, y, h]))
    loads = [
        pltpu.make_async_copy(src, dst, local_sems.at[i]) for i, (src, dst) in enumerate(loads)
    ]
    for load in loads:
        load.start()
    wall[z, c, 0:64, :] = jnp.zeros((64, HDIM), BF)
    wall[z, c, 0:SHARD_ROWS, :] = kw[...]
    wall[z, c, PAD_ROWS : PAD_ROWS + SHARD_ROWS, :] = vw[...]

    rows_iota = lax.broadcasted_iota(jnp.int32, (512, 512), 0)
    spread[...] = jnp.where(rows_iota == place[...], 1.0, 0.0).astype(BF)
    loads[0].wait()
    r_iota = lax.broadcasted_iota(jnp.int32, (32, 512), 0)
    s_iota = lax.broadcasted_iota(jnp.int32, (32, 512), 1)
    picked = low * 16 + r_iota + jnp.where(r_iota >= 16, 240, 0)
    pick = jnp.where(s_iota == picked, 1.0, 0.0).astype(BF)
    chosen = dot(pick, spread[...], 1, 1).astype(BF)
    relayed[...] = dot(chosen, encs[...]).astype(BF).reshape(2, 16, ENC)
    for load in loads[1:]:
        load.wait()
    stores = []

    def store(src, dst):
        copy = pltpu.make_async_copy(src, dst, local_sems.at[8 + len(stores)])
        copy.start()
        stores.append(copy)

    pl.semaphore_wait(barrier, len(peers) + 2 - jnp.where(self_half < 2, 1, 0))

    def gather1(a, wide):
        send, rest = sem(), sem()
        finals.append((wide, send))
        ahead = [sem() for _ in range(3)]
        across = [sem() for _ in range(3)]
        block0, block1 = a.at[x, y, 0], a.at[x, y, 1]
        for i, k in enumerate((1, 3, 2)):
            push(block0, block0, at(dx=k), send, ahead[i])
            push(block1, block1, at(dy=k), send, across[i])
        for k in (1, 3, 2):
            push(block0, block0, at(dy=k), send, rest)
            push(block1, block1, at(dx=k), send, rest)
        return send, rest, ahead, across

    def gather2(a, first):
        send, rest, ahead, across = first
        for i, k in enumerate((1, 3, 2)):
            block = a.at[(x + 4 - k) % 4, y, 0]
            drain(block, ahead[i])
            for j in (1, 3, 2):
                push(block, block, at(dy=j), send, rest)
            block = a.at[x, (y + 4 - k) % 4, 1]
            drain(block, across[i])
            for j in (1, 3, 2):
                push(block, block, at(dx=j), send, rest)
        return a.at[pl.ds(0, 3)], rest

    def landed(end):
        drain(*end)

    pieces = ((0, 64), (64, 128), (192, 128))
    limits = ((8, 7), (7, 8), (8, 7))
    strides = (2, 2, 2)
    arriving = [{k: sem() for k in range(1, 9)} for _ in pieces]
    sending = [sem() for _ in pieces]
    for (start, rows), one in zip(pieces, sending):
        finals.append((wall.at[pl.ds(0, 15), 0, pl.ds(start, rows)], one))

    def forward(p, j):
        start, rows = pieces[p]
        base = strides[p] * j
        for step in range(strides[p], 0, -1):
            k = base + step
            for side, sign in enumerate((1, -1)):
                if k <= limits[p][side]:
                    block = wall.at[(z - sign * base + 16) % 16, c, pl.ds(start, rows)]
                    push(block, block, at(dz=sign * step), sending[p], arriving[p][k])

    crossing = [(sem(), sem()) for _ in pieces]
    for (start, rows), one in zip(pieces, crossing):
        finals.append((wall.at[:, 0, pl.ds(start, rows)], one[0]))

    def to_sibling(p, *ks):
        start, rows = pieces[p]
        for k in ks:
            for dz in both(k):
                block = wall.at[(z + dz + 16) % 16, c, pl.ds(start, rows)]
                push(block, block, at(dc=1), *crossing[p])

    def all_crossed(p):
        start, rows = pieces[p]
        drain(wall.at[:, 0, pl.ds(start, rows)], crossing[p][1])

    def wait_blocks(p, *ks):
        start, rows = pieces[p]
        for k in ks:
            drain(wall.at[pl.ds(0, len(both(k))), 0, pl.ds(start, rows)], arriving[p][k])

    def pass_on(p, j):
        wait_blocks(p, strides[p] * j)
        forward(p, j)
        to_sibling(p, strides[p] * j)

    def hand_over(p, *ks):
        for k in ks:
            wait_blocks(p, k)
            to_sibling(p, k)

    def both(k):
        return (k, -k) if 0 < k < 8 else (k,)

    def relay(source, target, pair):
        sends, recvs = pair
        for half in range(2):
            peer = low + 16 * half

            @pl.when(self_half == half)
            def _():
                pltpu.make_async_copy(source.at[half], target, recvs.at[d // 16]).start()

            @pl.when(self_half != half)
            def _():
                push(source.at[half], target, (peer, m), sends.at[half], recvs.at[d // 16])

    def relay_landed(source, target, pair):
        sends, recvs = pair
        for half in range(2):
            drain(target(half), recvs.at[half])

            @pl.when(self_half != half)
            def _():
                drain(source.at[half], sends.at[half])

    def two():
        count[0] += 2
        return sems.at[pl.ds(count[0] - 2, 2)]

    pair_a = two(), two()
    forward(0, 0)
    relay(relayed, earr.at[x, y, d // 16], pair_a)
    forward(1, 0)
    f1 = gather1(feats, many)
    forward(2, 0)
    g1 = gather1(gins, many)
    for p in range(3):
        to_sibling(p, 0)

    order = omap[...]
    source = order >> 4
    rank = (((source + d) & 15) << 5) + ((source >> 4) << 4) + (order & 15)
    spread_o = jnp.where(rows_iota == rank, 1.0, 0.0).astype(BF)

    e_iota = lax.broadcasted_iota(jnp.int32, (ENC, 1024), 0)
    p_iota = lax.broadcasted_iota(jnp.int32, (ENC, 1024), 1)
    within = p_iota & 31
    select = jnp.where(
        (within < SHARD_ROWS) & ((p_iota >> 5) * SHARD_ROWS + within == e_iota), 1.0, 0.0
    ).astype(BF)

    pass_on(0, 1)
    hand_over(0, 1)
    pass_on(1, 1)
    pass_on(2, 1)
    relay_landed(relayed, lambda half: earr.at[x, y, half], pair_a)
    e1 = gather1(earr, many_e)
    hand_over(1, 1)
    f2 = gather2(feats, f1)
    hand_over(2, 1)
    pass_on(0, 2)
    hand_over(0, 3)
    pass_on(1, 2)
    e2 = gather2(earr, e1)
    g2 = gather2(gins, g1)
    pass_on(2, 2)
    hand_over(1, 3)
    hand_over(2, 3)
    pass_on(0, 3)
    hand_over(0, 5)
    pass_on(1, 3)
    pass_on(2, 3)
    hand_over(1, 5)
    hand_over(0, 8)
    hand_over(2, 5)
    hand_over(0, 7)
    all_crossed(0)

    padded = jnp.concatenate(
        [
            wall[:, :, 0:32, :].reshape(1024, HDIM),
            wall[:, :, 32:64, :].reshape(1024, HDIM),
        ],
        1,
    )
    kv_weight = dot(select, padded).astype(BF)
    landed(e2)
    arrived = earr[...].reshape(512, ENC)
    kv_arrived = dot(arrived, kv_weight).astype(BF)
    kvs[256:768, :] = dot(spread_o, kv_arrived, 0, 0).astype(BF)
    shift = sem(), sem()
    finals.append((kvs.at[pl.ds(0, 256)], shift[0]))
    push(kvs.at[pl.ds(512, 256)], kvs.at[pl.ds(0, 256)], after, *shift)

    hand_over(1, 8)
    hand_over(2, 8)
    hand_over(1, 7)
    hand_over(2, 7)

    def block_of(a, i):
        return a[i // 4, i % 4].reshape(128, 256)

    def wq(i):
        return wall[i, :, 64:192, :].reshape(256, HDIM)

    def wo(i):
        return jnp.concatenate([wall[i, 0, 192:320, :], wall[i, 1, 192:320, :]], 1)

    landed(f2)
    all_crossed(1)
    queries = jnp.zeros((128, HDIM), F32)
    for i in range(16):
        queries += dot(block_of(feats, i), wq(i))
    queries = queries.astype(BF)
    drain(kvs.at[pl.ds(0, 256)], shift[1])
    keys = kvs[:, 0:HDIM]
    values = kvs[:, HDIM:]
    token = lax.broadcasted_iota(jnp.int32, (128, 768), 0)
    column = lax.broadcasted_iota(jnp.int32, (128, 768), 1)
    stretch = jnp.where(token >= 63, 1, 0) + jnp.where(token >= 127, 1, 0)
    first = jnp.where(d % 16 == 0, 1, 0)
    mask = ((column >> 8) == stretch) & (stretch >= first)
    scores = jnp.where(mask, dot(queries, keys, 1, 1) * SCALE, -1e30)
    top = jnp.max(scores, -1, keepdims=True)
    expo = jnp.where(mask, jnp.exp(scores - top), 0.0)
    total = jnp.sum(expo, -1, keepdims=True)
    probs = expo / jnp.where(total > 0.0, total, 1.0)
    probs_half = probs.astype(BF)
    attended = dot(probs_half, values).astype(BF)
    landed(g2)
    all_crossed(2)
    d_att = jnp.zeros((128, HDIM), F32)
    for i in range(16):
        d_att += dot(block_of(gins, i), wo(i), 1, 1)
    d_att = d_att.astype(BF)
    grad_probs = dot(d_att, values, 1, 1)
    grad_scores = (
        probs * (grad_probs - jnp.sum(probs * grad_probs, -1, keepdims=True))
    ).astype(BF)
    key_terms = dot(grad_scores, queries, 0, 0) * SCALE
    value_terms = dot(probs_half, d_att, 0, 0)
    pair_terms = jnp.concatenate([key_terms, value_terms], 1)
    cbuf[...] = pair_terms[0:256].astype(BF)
    carry = sem(), sem()
    finals.append((cbuf, carry[0]))
    push(cbuf, crecv, before, *carry)
    grad_queries = (dot(grad_scores, keys) * SCALE).astype(BF)

    def scatter1(a, land, wide):
        send, recv = sem(), sem()
        finals.append((wide, send))
        for k in (1, 3, 2):
            push(a.at[(x + k) % 4, :, 0], land.at[0, k - 1], at(dx=k), send, recv)
            push(a.at[:, (y + k) % 4, 1], land.at[1, k - 1], at(dy=k), send, recv)
        return send, recv

    def add_up(parts):
        total = parts[0].astype(F32)
        for part in parts[1:]:
            total = total + part.astype(F32)
        return total.astype(BF)

    def scatter2(a, land, half_sum, land2, first):
        send, recv = first
        drain(land, recv)
        half_sum[0] = add_up([a[x, :, 0]] + [land[0, k] for k in range(3)])
        half_sum[1] = add_up([a[:, y, 1]] + [land[1, k] for k in range(3)])
        recv = sem()
        for k in (1, 3, 2):
            push(half_sum.at[0, (y + k) % 4], land2.at[0, k - 1], at(dy=k), send, recv)
            push(half_sum.at[1, (x + k) % 4], land2.at[1, k - 1], at(dx=k), send, recv)
        return recv

    def scattered(half_sum, land2, recv):
        drain(land2, recv)
        return [
            add_up([half_sum[0, y]] + [land2[0, k] for k in range(3)]),
            add_up([half_sum[1, x]] + [land2[1, k] for k in range(3)]),
        ]

    def z_swap(t, s):
        send, recv = sem(), sem()
        finals.append((s, send))
        push(t.at[:, 1 - c], s, at(dc=1), send, recv)
        return recv

    def z_odd(t, s, u, odd, chain, swap, sign):
        drain(s, swap)
        for k in range(16):
            there = (z + sign * k + 16) % 16
            u[(k % 2) * 8 + k // 2] = add_up([t[there, c], s[there]])
        send, recv = sem(), sem()
        finals.append((u.at[pl.ds(0, 15)], send))
        push(u.at[4], chain.at[0, 3], at(dz=2 * sign), send, recv)
        push(u.at[pl.ds(8, 4)], odd.at[0], at(dz=sign), send, recv)
        push(u.at[pl.ds(12, 4)], odd.at[1], at(dz=-sign), send, recv)
        return send, recv, u.at[pl.ds(0, 9)]

    def z_chain(u, odd, chain, out, step, sign, j):
        send, recv, size = step
        drain(size, recv)
        ahead = [u[j], odd[0, j], chain[0, j]]
        behind = [u[8 - j], odd[1, 3 - j]]
        if j < 3:
            behind.append(chain[1, j])
        out[0, j] = add_up(ahead)
        out[1, j] = add_up(behind)
        recv = sem()
        push(out.at[0, j], chain.at[0, j - 1], at(dz=2 * sign), send, recv)
        push(out.at[1, j], chain.at[1, j - 1], at(dz=-2 * sign), send, recv)
        return send, recv, u.at[pl.ds(0, 2)]

    def z_end(u, odd, chain, step):
        drain(step[2], step[1])
        return add_up([u[0], odd[0, 0], odd[1, 3], chain[0, 0], chain[1, 0]])

    for i in range(16):
        part = dot(attended, wo(i)).astype(BF)
        lp[i // 4, i % 4] = part.reshape(2, 64, 256)
    lp1 = scatter1(lp, rs1.at[0], many)
    for i in range(16):
        part = dot(attended, block_of(gins, i), 0, 0).astype(BF)
        tz[0, i, 0] = part[:, 0:HDIM]
        tz[0, i, 1] = part[:, HDIM:]
    out_swap = z_swap(tz.at[0], sib.at[0])
    drain(crecv, carry[1])
    pair_own = jnp.concatenate(
        [pair_terms[256:512], pair_terms[512:768] + crecv[...].astype(F32)], 0
    ).astype(BF)
    pair_arr = dot(spread_o, pair_own).astype(BF)
    ep[...] = dot(pair_arr, kv_weight, 1, 1).astype(BF).reshape(4, 4, 2, 16, ENC)
    ep1 = scatter1(ep, rs1e, many_e)
    for i in range(16):
        part = dot(grad_queries, wq(i), 1, 1).astype(BF)
        ip[i // 4, i % 4] = part.reshape(2, 64, 256)
    ip1 = scatter1(ip, rs1.at[1], many)
    for i in range(16):
        part = dot(block_of(feats, i), grad_queries, 0, 0).astype(BF)
        tz[1, i] = part.reshape(2, 128, HDIM)
    query_swap = z_swap(tz.at[1], sib.at[1])
    pair_part = dot(arrived, pair_arr, 0, 0).astype(BF)
    tzk[...] = dot(select, pair_part, 0, 0).astype(BF).reshape(16, 2, 32, 256)
    pair_swap = z_swap(tzk, sibk)

    zs = [
        (uz.at[0], rodd.at[0], rch.at[0], chs.at[0], 1),
        (uz.at[1], rodd.at[1], rch.at[1], chs.at[1], -1),
        (uzk, roddk, rchk, chsk, 1),
    ]
    steps = [
        z_odd(tz.at[0], sib.at[0], uz.at[0], rodd.at[0], rch.at[0], out_swap, 1),
        z_odd(tz.at[1], sib.at[1], uz.at[1], rodd.at[1], rch.at[1], query_swap, -1),
        z_odd(tzk, sibk, uzk, roddk, rchk, pair_swap, 1),
    ]

    def z_all(j):
        for i, (u, odd, chain, out, sign) in enumerate(zs):
            steps[i] = z_chain(u, odd, chain, out, steps[i], sign, j)

    lp2 = scatter2(lp, rs1.at[0], mid.at[0], rs2.at[0], lp1)
    ep2 = scatter2(ep, rs1e, mide, rs2e, ep1)
    z_all(3)
    halves = scattered(mid.at[0], rs2.at[0], lp2)
    for h in range(2):
        layer_out[x, y, h] = halves[h]
    lo1 = gather1(layer_out, many)
    halves = scattered(mide, rs2e, ep2)
    for h in range(2):
        eout[h] = halves[h]
    pair_b = two(), two()
    relay(eout, hall.at[x, y, d // 16], pair_b)
    ip2 = scatter2(ip, rs1.at[1], mid.at[1], rs2.at[1], ip1)
    z_all(2)
    lo2 = gather2(layer_out, lo1)
    relay_landed(eout, lambda half: hall.at[x, y, half], pair_b)
    h1 = gather1(hall, many_e)
    z_all(1)
    halves = scattered(mid.at[1], rs2.at[1], ip2)
    for h in range(2):
        input_grad[64 * h : 64 * h + 64, :] = halves[h]
    store(input_grad, input_hbm)
    h2 = gather2(hall, h1)
    out_grad[...] = z_end(uz.at[0], rodd.at[0], rch.at[0], steps[0])
    store(out_grad, out_hbm)
    query_grad[...] = z_end(uz.at[1], rodd.at[1], rch.at[1], steps[1])
    store(query_grad, query_hbm)
    pair_grad[...] = z_end(uzk, roddk, rchk, steps[2])
    store(pair_grad, pair_hbm)
    landed(lo2)
    for i in range(16):
        flat[:, 256 * i : 256 * i + 256] = block_of(layer_out, i)
    store(flat, layer_hbm)
    landed(h2)
    for i in range(16):
        for half in range(2):
            owner = (i - d + 32) % 16 + 16 * half
            sorted_enc[pl.ds(pl.multiple_of(owner * 16, 16), 16), :] = hall[i // 4, i % 4, half]
    enc_grad[...] = dot(spread[...], sorted_enc[...]).astype(BF)
    store(enc_grad, enc_hbm)
    for copy in stores:
        copy.wait()
    for end in finals:
        drain(*end)
    assert count[0] == N_SEMS, count[0]


def finish(
    layer, input_g, query_g, pair_g, out_g, enc_g,
    layer_out, input_out, query_out, key_out, value_out, out_out, enc_out,
    held_l, held_i, held_q, held_p, held_o, held_e, sems,
):
    pairs = []
    for i in range(4):
        for src, held, dst, rows in (
            (layer, held_l, layer_out, 32),
            (enc_g, held_e, enc_out, 128),
        ):
            span = pl.ds(rows * i, rows)
            pairs.append((src.at[span], held.at[span], dst.at[span]))
    pairs += [
        (input_g, held_i, input_out),
        (query_g, held_q, query_out),
        (out_g, held_o, out_out),
    ]
    ins = [
        pltpu.make_async_copy(src, held, sems.at[i]) for i, (src, held, _) in enumerate(pairs)
    ]
    outs = [
        pltpu.make_async_copy(held, dst, sems.at[12 + i])
        for i, (_, held, dst) in enumerate(pairs)
    ]
    pair_in = pltpu.make_async_copy(pair_g, held_p, sems.at[11])
    pair_in.start()
    for copy in ins:
        copy.start()
    pair_in.wait()
    key_out[...] = held_p[0:SHARD_ROWS, 0:HDIM]
    value_out[...] = held_p[0:SHARD_ROWS, HDIM:]
    for copy, onward in zip(ins, outs):
        copy.wait()
        onward.start()
    for copy in outs:
        copy.wait()


def shards(
    tokens,
    encodings,
    shard_place,
    owner_map,
    query_weight,
    key_weight,
    value_weight,
    out_weight,
    grad_out,
):
    vmem = pl.BlockSpec(memory_space=pltpu.VMEM)
    hbm = pl.BlockSpec(memory_space=pl.ANY)
    outs = [
        jax.ShapeDtypeStruct((128, 4096), BF),
        jax.ShapeDtypeStruct((128, 256), BF),
        jax.ShapeDtypeStruct((128, 128), BF),
        jax.ShapeDtypeStruct((32, 256), BF),
        jax.ShapeDtypeStruct((128, 128), BF),
        jax.ShapeDtypeStruct((512, ENC), BF),
    ]
    shapes = [
        (512, ENC),
        (128, 4096),
        (4, 4, 2, 64, 256),
        (128, 256),
        (128, 128),
        (32, 256),
        (128, 128),
        (512, ENC),
        (4, 4, 2, 64, 256),
        (4, 4, 2, 64, 256),
        (16, 2, 320, 128),
        (512, 512),
        (512, ENC),
        (2, 16, ENC),
        (4, 4, 2, 16, ENC),
        (768, 256),
        (4, 4, 2, 64, 256),
        (4, 4, 2, 64, 256),
        (4, 4, 2, 16, ENC),
        (2, 2, 3, 4, 64, 256),
        (2, 3, 4, 16, ENC),
        (2, 2, 3, 64, 256),
        (2, 3, 16, ENC),
        (2, 2, 4, 64, 256),
        (2, 4, 16, ENC),
        (2, 16, 2, 128, 128),
        (16, 2, 32, 256),
        (2, 16, 128, 128),
        (16, 32, 256),
        (2, 16, 128, 128),
        (16, 32, 256),
        (2, 2, 4, 128, 128),
        (2, 4, 32, 256),
        (2, 2, 4, 128, 128),
        (2, 4, 32, 256),
        (2, 2, 4, 128, 128),
        (2, 4, 32, 256),
        (256, 256),
        (256, 256),
        (2, 16, ENC),
        (4, 4, 2, 16, ENC),
        (30, 64, 256),
        (30, 16, ENC),
    ]
    scratch = [pltpu.VMEM(shape, BF) for shape in shapes]
    scratch += [
        pltpu.SemaphoreType.DMA((N_SEMS,)),
        pltpu.SemaphoreType.DMA((14,)),
    ]
    parts = pl.pallas_call(
        kernel,
        out_shape=outs,
        in_specs=[hbm] * 4 + [vmem] * 2 + [hbm] + [vmem] * 2,
        out_specs=[hbm] * 6,
        scratch_shapes=scratch,
        compiler_params=pltpu.CompilerParams(
            collective_id=0, has_side_effects=True, vmem_limit_bytes=56 * 1024 * 1024
        ),
        name="retro",
    )(
        tokens,
        grad_out,
        query_weight,
        out_weight,
        key_weight,
        value_weight,
        encodings,
        shard_place,
        owner_map,
    )
    shapes = [
        (128, 4096),
        (128, 256),
        (128, 128),
        (SHARD_ROWS, 128),
        (SHARD_ROWS, 128),
        (128, 128),
        (512, ENC),
    ]
    return pl.pallas_call(
        finish,
        out_shape=[jax.ShapeDtypeStruct(shape, BF) for shape in shapes],
        in_specs=[hbm] * 6,
        out_specs=[hbm] * 3 + [vmem] * 2 + [hbm] * 2,
        scratch_shapes=[
            pltpu.VMEM((128, 4096), BF),
            pltpu.VMEM((128, 256), BF),
            pltpu.VMEM((128, 128), BF),
            pltpu.VMEM((32, 256), BF),
            pltpu.VMEM((128, 128), BF),
            pltpu.VMEM((512, ENC), BF),
            pltpu.SemaphoreType.DMA((23,)),
        ],
        name="finish",
    )(*parts)


def solution(mesh):
    placed = (
        P("dp", "mp"),
        P("dp", None),
        P("dp", None),
        P("dp", None),
        P("dp", "mp"),
        P("dp", "mp"),
        P("dp", "mp"),
        P("mp", "dp"),
        P("dp", "mp"),
    )
    return jax.shard_map(
        shards,
        mesh=mesh,
        in_specs=placed,
        out_specs=(
            P("dp", None),
            P("dp", "mp"),
            P("dp", "mp"),
            P("dp", "mp"),
            P("dp", "mp"),
            P("mp", "dp"),
            P("dp", None),
        ),
        check_vma=False,
    )
```
